32 devices in a mesh: wide: 4 (over z), qa: 4 (over y, x), qb: 2 (over core).
Axes of the slice: x: 2, y: 2, z: 4, core: 2. Of those that a mesh axis runs over, the one named last changes fastest.
Arguments:
- core_slices: float32 [32768, 256], P(('wide', 'qa', 'qb')), may hold values from -64 to 64
- next_core: float32 [256, 16384], P('wide', ('qa', 'qb')), may hold values from -0.375 to 0.375
Outputs:
- ortho_basis: float32 [32768, 256], P(('wide', 'qa', 'qb'))
- new_core: float32 [256, 16384], P('wide', ('qa', 'qb'))
The draws below stay inside these ranges and needn't reach their ends.
All inputs are finite; a program needn't handle non-finite values.
Results may differ from the reference program's by a relative error of at most 0.0003.
Values sent between devices are 32-bit elements; how exact they have to be, the bound alone decides.
A program may use at most 128 MiB of HBM per device.

```python
import jax
import jax.numpy as jnp
from jax import lax

RANK = 256
ROWS_DEV = 1024
NEXT_COLS = 16384
ROWS = 32768


def draw_core_slices(key, part):
    keys = jax.random.split(jax.random.fold_in(key, 7), 4)
    block_rows = min(256, ROWS_DEV)
    blocks = ROWS // block_rows
    row_scale = jnp.repeat(10.0 ** jax.random.uniform(keys[0], (blocks, 1), jnp.float32), block_rows, axis=0)
    rank_order = jax.random.permutation(keys[1], RANK).astype(jnp.float32)
    spread = 10.0 ** (-2.75 * rank_order / (RANK - 1))
    positions = jnp.arange(RANK, dtype=jnp.float32)
    cosine = jnp.sqrt(2.0 / RANK) * jnp.cos(jnp.pi * (2.0 * positions[None, :] + 1.0) * positions[:, None] / (2.0 * RANK))
    cosine = cosine * jnp.where(positions[:, None] == 0.0, jnp.sqrt(0.5), 1.0)
    sign_flips = jnp.where(jax.random.bernoulli(keys[2], 0.5, (1, RANK)), 1.0, -1.0)
    mixing = spread[:, None] * cosine * sign_flips
    values = jnp.clip(jax.random.normal(keys[3], (ROWS, RANK), jnp.float32), -4.0, 4.0)
    mixed_rows = jnp.dot(values, mixing, precision=lax.Precision.HIGHEST, preferred_element_type=jnp.float32)
    return jnp.clip(mixed_rows * row_scale, -64.0, 64.0).astype(jnp.float32)


def block_scale(key, shape, cuts, low, largest):
    def one(dim, parts):
        steps = jax.random.uniform(jax.random.fold_in(jax.random.fold_in(key, 6), dim), (parts,), jnp.float32, low / len(cuts), largest / len(cuts))
        return jnp.repeat(jnp.exp(steps), shape[dim] // parts).reshape((-1,) + (1,) * (len(shape) - dim - 1))

    gain = one(*cuts[0])
    for cut in cuts[1:]:
        gain = gain * one(*cut)
    return gain


def gaussian(stream_key, extent, scale, bound, cuts=(), kind=jnp.bfloat16):
    array = scale * jax.random.normal(stream_key, extent, jnp.float32)
    if cuts:
        array = array * block_scale(stream_key, extent, cuts, -0.22, 0.18)
    return jnp.clip(array, -bound, bound).astype(kind)


def setup_inputs(seed: int = 0) -> dict:
    streams_of = jax.random.split(jax.random.key(seed), 3)
    return {
        "core_slices": draw_core_slices(jax.random.fold_in(streams_of[2], 71), 0),
        "next_core": gaussian(streams_of[1], (RANK, NEXT_COLS), RANK ** -0.5, 0.375, ((0, 4), (1, 8)), jnp.float32),
    }


def leaf_parts(gram):
    count = gram.shape[0]
    places = jnp.arange(count)
    work = gram
    lower = jnp.zeros_like(gram)
    for k in range(count):
        column = work[:, k]
        column = jnp.where(places >= k, column / jnp.sqrt(column[k]), jnp.zeros_like(column))
        work = work - column[:, None] * column[None, :]
        lower = lower.at[:, k].set(column)
    inverse = jnp.zeros_like(gram)
    for k in range(count):
        row = lower[k]
        earlier = jnp.where(places < k, row, jnp.zeros_like(row))
        unit = jnp.where(places == k, jnp.ones_like(row), jnp.zeros_like(row))
        carried = jnp.dot(earlier, inverse, precision=lax.Precision.HIGHEST, preferred_element_type=gram.dtype)
        inverse = inverse.at[k].set((unit - carried) / row[k])
    return (lower, inverse)

def lower_parts(gram):
    count = gram.shape[0]
    if count <= 16:
        return leaf_parts(gram)
    half = count // 2
    lower_top, inverse_top = lower_parts(gram[:half, :half])
    lower_side = jnp.dot(gram[half:, :half], inverse_top.T, precision=lax.Precision.HIGHEST, preferred_element_type=gram.dtype)
    schur = gram[half:, half:] - jnp.dot(lower_side, lower_side.T, precision=lax.Precision.HIGHEST, preferred_element_type=gram.dtype)
    lower_end, inverse_end = lower_parts(schur)
    inverse_side = -jnp.dot(jnp.dot(inverse_end, lower_side, precision=lax.Precision.HIGHEST, preferred_element_type=gram.dtype), inverse_top, precision=lax.Precision.HIGHEST, preferred_element_type=gram.dtype)
    zeros_block = jnp.zeros((half, count - half), gram.dtype)
    lower = jnp.concatenate([jnp.concatenate([lower_top, zeros_block], axis=1), jnp.concatenate([lower_side, lower_end], axis=1)], axis=0)
    inverse = jnp.concatenate([jnp.concatenate([inverse_top, zeros_block], axis=1), jnp.concatenate([inverse_side, inverse_end], axis=1)], axis=0)
    return (lower, inverse)

def upper_factor(gram):
    lower, inverse_lower = lower_parts(gram)
    return (lower.T, inverse_lower.T)

def reference(core_slices, next_core):
    halved = core_slices.astype(jnp.bfloat16)
    first_gram = lax.dot_general(halved, halved, (((0,), (0,)), ((), ())), preferred_element_type=jnp.float32) / ROWS
    upper_one, inverse_one = upper_factor(first_gram)
    section_one = jnp.dot(core_slices, inverse_one, precision=lax.Precision.HIGHEST, preferred_element_type=jnp.float32)
    second_gram = lax.dot_general(section_one, section_one, (((0,), (0,)), ((), ())), precision=lax.Precision.HIGHEST, preferred_element_type=jnp.float32) / ROWS
    upper_two, inverse_two = upper_factor(second_gram)
    ortho_basis = jnp.dot(section_one, inverse_two, precision=lax.Precision.HIGHEST, preferred_element_type=jnp.float32)
    factor = jnp.dot(upper_two, upper_one, precision=lax.Precision.HIGHEST, preferred_element_type=jnp.float32)
    new_core = jnp.dot(factor, next_core, precision=lax.Precision.HIGHEST, preferred_element_type=jnp.float32)
    return (ortho_basis, new_core)
```

```python
import functools

import jax
import jax.numpy as jnp
from jax import lax
from jax.experimental import pallas as pl
from jax.experimental.pallas import tpu as pltpu
from jax.sharding import PartitionSpec as P

AXES = ("wide", "qa", "qb")
STRIP = 8
LANES = 128
PANEL = 32
HIGHEST = lax.Precision.HIGHEST
VMEM_LIMIT = 40 * 1024 * 1024


def mm(a, b, dims):
    return lax.dot_general(
        a, b, (dims, ((), ())), precision=HIGHEST, preferred_element_type=jnp.float32
    )


def forward(items, below, inverse_diag):
    done = []
    for j in range(STRIP):
        value = items[j]
        for m in range(j):
            value = value - below[j, m] * done[m]
        done.append(value * inverse_diag[j])
    return done


def factor_in_place(work, upper):
    n = work.shape[0]
    tiles = n // LANES

    def wide(value):
        return jnp.concatenate([value] * tiles, axis=1) if tiles > 1 else value

    lane = lax.broadcasted_iota(jnp.int32, (STRIP, n), 1)
    sub = lax.broadcasted_iota(jnp.int32, (STRIP, n), 0)

    def stack(rows):
        out = rows[0]
        for i in range(1, STRIP):
            out = jnp.where(sub == i, rows[i], out)
        return out

    for p in range(0, n, PANEL):
        count = PANEL // STRIP
        strips = [work[p + STRIP * s : p + STRIP * (s + 1), :] for s in range(count)]
        uppers, fulls = [], []
        for s in range(count):
            k = p + STRIP * s
            here = strips[s]
            inside = (lane >= k) & (lane < k + STRIP)
            spread = [jnp.broadcast_to(here[i : i + 1, :], (STRIP, n)) for i in range(STRIP)]
            a = {}
            for j in range(STRIP):
                for i in range(j, STRIP):
                    a[i, j] = jnp.broadcast_to(
                        spread[j][:, k + i : k + i + 1], (STRIP, LANES)
                    )
            below, inverse_diag = {}, []
            for j in range(STRIP):
                d = a[j, j]
                r = lax.rsqrt(d)
                r = r * (1.5 - 0.5 * d * r * r)
                inverse_diag.append(r)
                for i in range(j + 1, STRIP):
                    below[i, j] = a[i, j] * r
                for i in range(j + 1, STRIP):
                    for m in range(j + 1, i + 1):
                        a[i, m] = a[i, m] - below[i, j] * below[m, j]
            below_w = {key: wide(value) for key, value in below.items()}
            diag_w = [wide(value) for value in inverse_diag]
            u_rows = forward(spread, below_w, diag_w)
            x_rows = forward(
                [
                    jnp.where(inside, jnp.where(lane == k + i, 1.0, 0.0), spread[i])
                    for i in range(STRIP)
                ],
                below_w,
                diag_w,
            )
            full = stack(x_rows)
            uppers.append(jnp.where(lane >= k + sub, stack(u_rows), 0.0))
            fulls.append(jnp.where((lane >= k + STRIP) & (lane < p + PANEL), 0.0, full))
            for t in range(s + 1, count):
                other = strips[t]
                side = forward(
                    [
                        jnp.broadcast_to(other[:, k + j : k + j + 1], (STRIP, LANES))
                        for j in range(STRIP)
                    ],
                    below,
                    inverse_diag,
                )
                value = jnp.where(inside, 0.0, other)
                for j in range(STRIP):
                    value = value - wide(side[j]) * x_rows[j]
                strips[t] = value
        end = p + PANEL
        u_panel = jnp.concatenate(uppers, axis=0)
        x_panel = jnp.concatenate(fulls, axis=0)
        upper[p:end, :] = u_panel
        lane_panel = lax.broadcasted_iota(jnp.int32, (PANEL, n), 1)
        work[p:end, :] = jnp.where(lane_panel < end, x_panel, 0.0)
        if end < n:
            start = end // LANES * LANES
            update = mm(u_panel[:, start:], x_panel, ((0,), (0,)))[end - start :, :]
            rest_lane = lax.broadcasted_iota(jnp.int32, (n - end, n), 1)
            rest = work[end:, :]
            rest = jnp.where((rest_lane >= p) & (rest_lane < end), 0.0, rest)
            work[end:, :] = rest - update


def first_kernel(total_rows, core_ref, gram_ref, section_ref, part_ref, upper_ref, work):
    work[...] = gram_ref[...] / total_rows
    factor_in_place(work, upper_ref)
    section_ref[...] = mm(core_ref[...], work[...], ((1,), (1,)))
    part_ref[...] = mm(section_ref[...], section_ref[...], ((0,), (0,)))


def second_kernel(
    total_rows, section_ref, gram_ref, upper_one_ref, next_ref, ortho_ref, new_ref, work, upper
):
    rows, columns = new_ref.shape
    work[...] = gram_ref[...] / total_rows
    factor_in_place(work, upper)
    ortho_ref[...] = mm(section_ref[...], work[...], ((1,), (1,)))
    start = pl.multiple_of(lax.axis_index("wide") * rows, rows)
    mine = mm(upper[pl.ds(start, rows), :], upper_one_ref[...], ((1,), (0,)))
    tile = min(512, columns)
    for c in range(0, columns, tile):
        new_ref[:, c : c + tile] = mm(mine, next_ref[:, c : c + tile], ((1,), (0,)))


def vmem_specs(count):
    return [pl.BlockSpec(memory_space=pltpu.VMEM)] * count


def gram_total(part):
    return lax.psum(part, AXES)


def per_device(core_slices, next_core):
    rows, rank = core_slices.shape
    f32 = jnp.float32
    total_rows = rows * lax.axis_size("wide") * lax.axis_size("qa") * lax.axis_size("qb")
    square = jax.ShapeDtypeStruct((rank, rank), f32)
    block = jax.ShapeDtypeStruct((rows, rank), f32)
    params = pltpu.CompilerParams(vmem_limit_bytes=VMEM_LIMIT)
    gathered = lax.all_gather(next_core, "wide", axis=0, tiled=True)
    halved = core_slices.astype(jnp.bfloat16)
    first_gram = gram_total(
        lax.dot_general(halved, halved, (((0,), (0,)), ((), ())), preferred_element_type=f32)
    )
    section, part, upper_one = pl.pallas_call(
        functools.partial(first_kernel, total_rows),
        out_shape=(block, square, square),
        in_specs=vmem_specs(2),
        out_specs=tuple(vmem_specs(3)),
        scratch_shapes=[pltpu.VMEM((rank, rank), f32)],
        compiler_params=params,
        name="factor_one",
    )(core_slices, first_gram)
    second_gram = gram_total(part)
    ortho_basis, new_core = pl.pallas_call(
        functools.partial(second_kernel, total_rows),
        out_shape=(block, jax.ShapeDtypeStruct(next_core.shape, f32)),
        in_specs=vmem_specs(4),
        out_specs=tuple(vmem_specs(2)),
        scratch_shapes=[pltpu.VMEM((rank, rank), f32), pltpu.VMEM((rank, rank), f32)],
        compiler_params=params,
        name="factor_two",
    )(section, second_gram, upper_one, gathered)
    return ortho_basis, new_core


def solution(mesh):
    return jax.shard_map(
        per_device,
        mesh=mesh,
        in_specs=(P(AXES, None), P("wide", ("qa", "qb"))),
        out_specs=(P(AXES, None), P("wide", ("qa", "qb"))),
        check_vma=False,
    )
```
